32 devices in a mesh: grp: 2 (over x), gx: 16 (over z, y, core).
Axes of the slice: x: 2, y: 2, z: 4, core: 2. Of those that a mesh axis runs over, the one named last changes fastest.
Arguments:
- e_forward: float32 [3, 256, 32, 256], P(None, ('grp', 'gx')), parts along dimension 1, may hold values from -6 to 6
- h_forward: float32 [3, 256, 32, 256], P(None, ('grp', 'gx')), parts along dimension 1, may hold values from -6 to 6
- p_forward: float32 [3, 256, 32, 256], P(None, ('grp', 'gx')), parts along dimension 1, may hold values from -6 to 6
- j_forward: float32 [3, 256, 32, 256], P(None, ('grp', 'gx')), parts along dimension 1, may hold values from -6 to 6
- e_adjoint: float32 [3, 256, 32, 256], P(None, ('grp', 'gx')), parts along dimension 1, may hold values from -6 to 6
- h_adjoint: float32 [3, 256, 32, 256], P(None, ('grp', 'gx')), parts along dimension 1, may hold values from -6 to 6
- p_adjoint: float32 [3, 256, 32, 256], P(None, ('grp', 'gx')), parts along dimension 1, may hold values from -6 to 6
- j_adjoint: float32 [3, 256, 32, 256], P(None, ('grp', 'gx')), parts along dimension 1, may hold values from -6 to 6
- design: float32 [32, 32, 256], P(('grp', 'gx')), parts along dimension 0, may hold values from 0 to 1
- source_amp: float32 [32, 3], P('grp'), parts along dimension 0, may hold values from -6 to 6
- source_cell: int32 [32], P('grp'), parts along dimension 0, may hold values from 0 to 1048575
- monitor_cell: int32 [32], P('grp'), parts along dimension 0, may hold values from 0 to 1048575
- slab_start: int32 [2], P('grp'), parts along dimension 0, may hold values from 8 to 15
- radius: int32 [2], P('grp'), parts along dimension 0, may hold values from 1 to 4
Outputs:
- e_forward_next: float32 [3, 256, 32, 256], P(None, ('grp', 'gx')), parts along dimension 1
- h_forward_next: float32 [3, 256, 32, 256], P(None, ('grp', 'gx')), parts along dimension 1
- e_adjoint_next: float32 [3, 256, 32, 256], P(None, ('grp', 'gx')), parts along dimension 1
- h_adjoint_next: float32 [3, 256, 32, 256], P(None, ('grp', 'gx')), parts along dimension 1
- design_grad: float32 [32, 32, 256], P(('grp', 'gx')), parts along dimension 0
The draws below stay inside these ranges and needn't reach their ends.
There are 2 independent parts, one for each index of `grp`. The reference program is written for one: setup_inputs(seed, part) draws one part's arguments, and reference() takes and returns one part's arrays. A program takes and returns all parts, laid end to end along the dimension named above; each array names one. Nothing has to cross between parts.
Inputs may be any that keep to these rules, and one draw needn't show every extreme that they name: `slab_start`: the slab begins within planes 8 to 15 of the grid.
All inputs are finite; a program needn't handle non-finite values.
Results may differ from the reference program's by a relative error of at most 0.0003.
Values sent between devices are 32-bit elements; how exact they have to be, the bound alone decides.
A program may use at most 128 MiB of HBM per device.

```python
import jax
import jax.numpy as jnp
from jax import lax

CZ = 8
NX = 32
NY = 256
NSRC = 16
NMON = 16
RMAX = 4
NZ = 128
DZ = 16


def set_ends(entries, stream_key, smallest, largest):
    place = [jax.random.randint(jax.random.fold_in(stream_key, axis), (), 0, length) for axis, length in enumerate(entries.shape)]
    widest = entries.shape.index(max(entries.shape))
    neighbour = place[:widest] + [(place[widest] + 1) % entries.shape[widest]] + place[widest + 1:]
    return entries.at[tuple(place)].set(smallest).at[tuple(neighbour)].set(largest)


def shard_levels(stream_key, shape, split, least, largest):
    def one(dim, shards_of):
        steps = jax.random.uniform(jax.random.fold_in(jax.random.fold_in(stream_key, 6), dim), (shards_of,), jnp.float32, least / len(split), largest / len(split))
        return jnp.repeat(jnp.exp(steps), shape[dim] // shards_of).reshape((-1,) + (1,) * (len(shape) - dim - 1))

    gain = one(*split[0])
    for cut in split[1:]:
        gain = gain * one(*cut)
    return gain


def gaussian(stream_key, dims, scale, reach, cuts=(), kind=jnp.bfloat16):
    entries = scale * jax.random.normal(stream_key, dims, jnp.float32)
    if cuts:
        entries = entries * shard_levels(stream_key, dims, cuts, -0.22, 0.18)
    return jnp.clip(entries, -reach, reach).astype(kind)


def setup_inputs(seed: int = 0, part: int = 0) -> dict:
    key_list = jax.random.split(jax.random.key(seed), 15)
    own_keys = jax.random.split(jax.random.fold_in(key_list[14], part), 15)
    e_forward = gaussian(own_keys[0], (3, NZ, NX, NY), 1.0, 6.0, ((1, 16),), jnp.float32)
    h_forward = gaussian(own_keys[1], (3, NZ, NX, NY), 1.0, 6.0, ((1, 16),), jnp.float32)
    p_forward = gaussian(own_keys[2], (3, NZ, NX, NY), 1.0, 6.0, ((1, 16),), jnp.float32)
    j_forward = gaussian(own_keys[3], (3, NZ, NX, NY), 1.0, 6.0, ((1, 16),), jnp.float32)
    e_adjoint = gaussian(own_keys[4], (3, NZ, NX, NY), 1.0, 6.0, ((1, 16),), jnp.float32)
    h_adjoint = gaussian(own_keys[5], (3, NZ, NX, NY), 1.0, 6.0, ((1, 16),), jnp.float32)
    p_adjoint = gaussian(own_keys[6], (3, NZ, NX, NY), 1.0, 6.0, ((1, 16),), jnp.float32)
    j_adjoint = gaussian(own_keys[7], (3, NZ, NX, NY), 1.0, 6.0, ((1, 16),), jnp.float32)
    design = jnp.clip(1.0 * jax.random.uniform(own_keys[8], (DZ, NX, NY), jnp.float32) ** shard_levels(own_keys[8], (DZ, NX, NY), ((0, 16),), -0.2, 0.2), 0.0, 1.0)
    source_amp = gaussian(own_keys[9], (NSRC, 3), 1.0, 6.0, (), jnp.float32)
    source_cell = set_ends(jax.random.randint(own_keys[10], (NSRC,), 0, NZ * NX * NY), jax.random.fold_in(own_keys[10], 1), 0, (NZ * NX * NY) - 1).astype(jnp.int32)
    monitor_cell = set_ends(jax.random.randint(own_keys[11], (NMON,), 0, NZ * NX * NY), jax.random.fold_in(own_keys[11], 1), 0, (NZ * NX * NY) - 1).astype(jnp.int32)
    slab_start = jax.random.randint(own_keys[12], (1,), CZ, 2 * CZ).astype(jnp.int32)
    radius = jax.random.randint(own_keys[13], (1,), 1, RMAX + 1).astype(jnp.int32)
    return dict(e_forward=e_forward, h_forward=h_forward, p_forward=p_forward, j_forward=j_forward, e_adjoint=e_adjoint, h_adjoint=h_adjoint, p_adjoint=p_adjoint, j_adjoint=j_adjoint, design=design, source_amp=source_amp, source_cell=source_cell, monitor_cell=monitor_cell, slab_start=slab_start, radius=radius)


DT = 0.5
EPS_RANGE = 10.0
STRENGTH_BASE = 0.5
STRENGTH_RANGE = 3.0
DAMPING = 0.2
GAIN_FIELD = 0.25
HIGH = lax.Precision.HIGHEST


def band_matrix(count, radius):
    rows = jnp.arange(count, dtype=jnp.int32)
    dist = jnp.abs(rows[:, None] - rows[None, :])
    weights = jnp.maximum(radius + 1 - dist, 0).astype(jnp.float32)
    return weights / jnp.sum(weights, axis=1, keepdims=True)


def ahead(field, axis):
    count = field.shape[axis]
    rest = lax.slice_in_dim(field, 1, count, axis=axis)
    return jnp.concatenate([rest, jnp.zeros_like(lax.slice_in_dim(field, 0, 1, axis=axis))], axis)


def behind(field, axis):
    count = field.shape[axis]
    rest = lax.slice_in_dim(field, 0, count - 1, axis=axis)
    return jnp.concatenate([jnp.zeros_like(lax.slice_in_dim(field, 0, 1, axis=axis)), rest], axis)


def update_h(efield, hfield):
    ex, ey, ez = efield[0], efield[1], efield[2]
    curl_x = (ahead(ez, 2) - ez) - (ahead(ey, 0) - ey)
    curl_y = (ahead(ex, 0) - ex) - (ahead(ez, 1) - ez)
    curl_z = (ahead(ey, 1) - ey) - (ahead(ex, 2) - ex)
    return hfield - DT * jnp.stack([curl_x, curl_y, curl_z])


def update_e(efield, hnext, jnext, permittivity, drive):
    hx, hy, hz = hnext[0], hnext[1], hnext[2]
    curl_x = (hz - behind(hz, 2)) - (hy - behind(hy, 0))
    curl_y = (hx - behind(hx, 0)) - (hz - behind(hz, 1))
    curl_z = (hy - behind(hy, 1)) - (hx - behind(hx, 2))
    curl = jnp.stack([curl_x, curl_y, curl_z])
    return efield + (DT / permittivity)[None] * (curl - jnext + drive)


def update_j(jfield, pfield, efield, strength):
    return ((1.0 - DAMPING * DT / 2.0) * jfield + DT * (strength[None] * efield - pfield)) / (1.0 + DAMPING * DT / 2.0)


def smooth(wx, wy, planes):
    inner = jnp.einsum("ax,zxy->zay", wx, planes, precision=HIGH)
    return jnp.einsum("zay,by->zab", inner, wy, precision=HIGH)


def smooth_adjoint(wx, wy, planes):
    inner = jnp.einsum("ax,zab->zxb", wx, planes, precision=HIGH)
    return jnp.einsum("zxb,by->zxy", inner, wy, precision=HIGH)


def split_cells(cells):
    zz = cells // (NX * NY)
    rest = cells % (NX * NY)
    return zz, rest // NY, rest % NY


def reference(e_forward, h_forward, p_forward, j_forward, e_adjoint, h_adjoint, p_adjoint, j_adjoint, design, source_amp, source_cell, monitor_cell, slab_start, radius):
    start = slab_start[0]
    wx = band_matrix(NX, radius[0])
    wy = band_matrix(NY, radius[0])
    rho_slab = smooth(wx, wy, design)
    zero = jnp.zeros((), jnp.int32)
    rho = lax.dynamic_update_slice(jnp.zeros((NZ, NX, NY), jnp.float32), rho_slab, (start, zero, zero))
    permittivity = 1.0 + EPS_RANGE * rho
    strength = STRENGTH_BASE + STRENGTH_RANGE * rho
    zs, xs, ys = split_cells(source_cell)
    drive = jnp.zeros((3, NZ, NX, NY), jnp.float32).at[:, zs, xs, ys].add(source_amp.T)
    zm, xm, ym = split_cells(monitor_cell)
    probe = e_forward[:, zm, xm, ym]
    drive_adj = jnp.zeros((3, NZ, NX, NY), jnp.float32).at[:, zm, xm, ym].add(probe)
    hf = update_h(e_forward, h_forward)
    ha = update_h(e_adjoint, h_adjoint)
    jf = update_j(j_forward, p_forward, e_forward, strength)
    ja = update_j(j_adjoint, p_adjoint, e_adjoint, strength)
    ef = update_e(e_forward, hf, jf, permittivity, drive)
    ea = update_e(e_adjoint, ha, ja, permittivity, drive_adj)
    intersection = jnp.sum(ea * ((ef - e_forward) + GAIN_FIELD * ef), axis=0)
    intersection_slab = lax.dynamic_slice(intersection, (start, zero, zero), (DZ, NX, NY))
    design_grad = smooth_adjoint(wx, wy, intersection_slab)
    return ef, hf, ea, ha, design_grad
```

```python
import functools

import jax
import jax.numpy as jnp
from jax import lax
from jax.experimental import pallas as pl
from jax.experimental.pallas import tpu as pltpu
from jax.sharding import PartitionSpec as P

DT = 0.5
EPS_RANGE = 10.0
STRENGTH_BASE = 0.5
STRENGTH_RANGE = 3.0
DAMPING = 0.2
GAIN_FIELD = 0.25
MESH = pl.DeviceIdType.MESH
F32 = jnp.float32
BF16 = jnp.bfloat16
ANY = pl.BlockSpec(memory_space=pl.ANY)
SMEM = pl.BlockSpec(memory_space=pltpu.SMEM)
VMEM = pl.BlockSpec(memory_space=pltpu.VMEM)


def slot_range(me, n, depth):
    base = depth * (me - 1) - (depth - 1)
    return base, jnp.maximum(base, 0), jnp.minimum(base + 2 * depth - 1, n)


def holders(me, depth):
    first = me // depth + 1
    return first, first + 1, me % depth


def ahead(v, axis):
    size = v.shape[axis]
    pos = lax.broadcasted_iota(jnp.int32, v.shape, axis)
    return jnp.where(pos == size - 1, 0.0, pltpu.roll(v, size - 1, axis))


def behind(v, axis):
    pos = lax.broadcasted_iota(jnp.int32, v.shape, axis)
    return jnp.where(pos == 0, 0.0, pltpu.roll(v, 1, axis))


def triangle(size, radius):
    a = lax.broadcasted_iota(jnp.int32, (size, size), 0)
    b = lax.broadcasted_iota(jnp.int32, (size, size), 1)
    return jnp.maximum(radius + 1 - jnp.abs(a - b), 0).astype(F32).astype(BF16)


def row_sums(shape, axis, radius):
    pos = lax.broadcasted_iota(jnp.int32, shape, axis)
    low = jnp.maximum(radius - pos, 0)
    high = jnp.maximum(radius - (shape[axis] - 1 - pos), 0)
    whole = (radius + 1) * (radius + 1)
    low, high = low.astype(F32), high.astype(F32)
    return whole.astype(F32) - 0.5 * (low * (low + 1.0) + high * (high + 1.0))


def halves(v):
    big = v.astype(BF16)
    return big, (v - big.astype(F32)).astype(BF16)


def band_product(plane, radius):
    nx, ny = plane.shape
    tx, ty = triangle(nx, radius), triangle(ny, radius)
    big, small = halves(plane)
    both = jnp.dot(jnp.concatenate([big, small], 0), ty, preferred_element_type=F32)
    big, small = halves(both[:nx] + both[nx:])
    return jnp.dot(tx, big, preferred_element_type=F32) + jnp.dot(
        tx, small, preferred_element_type=F32
    )


def inverse_sums(shape, radius):
    return 1.0 / (row_sums(shape, 0, radius) * row_sums(shape, 1, radius))


def exchange_kernel(
    n,
    radius_ref,
    design_ref,
    ef,
    ea,
    hf,
    ha,
    below_ref,
    above_ref,
    slots_ref,
    eb,
    hb,
    part,
    rho,
    load_sem,
    send_sem,
    up_send,
    up_recv,
    down_send,
    down_recv,
    slot_recv,
    self_sem,
):
    me = lax.axis_index("gx")
    depth = ef.shape[1]
    loads = []
    for r, (e, h) in enumerate(((ef, hf), (ea, ha))):
        loads.append(pltpu.make_async_copy(e.at[:, depth - 1], eb.at[r], load_sem.at[r, 0]))
        loads.append(pltpu.make_async_copy(h.at[0:2, depth - 1], hb.at[r], load_sem.at[r, 1]))
    for load in loads:
        load.start()

    barrier = pltpu.get_barrier_semaphore()

    @pl.loop(1, n)
    def _(k):
        pl.semaphore_signal(
            barrier, inc=1, device_id={"gx": lax.rem(me + k, n)}, device_id_type=MESH
        )

    radius = radius_ref[0]
    plane = design_ref[0]
    rho[...] = band_product(plane, radius) * inverse_sums(plane.shape, radius)
    pl.semaphore_wait(barrier, n - 1)

    first, second, shift = holders(me, depth)

    def to_holder(which, holder):
        slot = me - (depth * (holder - 1) - (depth - 1))
        return pltpu.make_async_remote_copy(
            src_ref=rho,
            dst_ref=slots_ref.at[slot],
            send_sem=send_sem.at[which],
            recv_sem=slot_recv.at[slot],
            device_id={"gx": holder},
            device_id_type=MESH,
        )

    def to_self(holder):
        slot = me - (depth * (holder - 1) - (depth - 1))
        return pltpu.make_async_copy(rho, slots_ref.at[slot], self_sem)

    def each_holder(remote, local):
        for which, holder, used in ((0, first, shift >= 0), (1, second, shift != 0)):
            pl.when(used & (holder != me))(functools.partial(remote, which, holder))
            pl.when(used & (holder == me))(functools.partial(local, holder))

    def to_below(r, e):
        return pltpu.make_async_remote_copy(
            src_ref=e.at[0:2, 0],
            dst_ref=above_ref.at[r],
            send_sem=down_send.at[r],
            recv_sem=down_recv.at[r],
            device_id={"gx": me - 1},
            device_id_type=MESH,
        )

    def to_above():
        return pltpu.make_async_remote_copy(
            src_ref=part,
            dst_ref=below_ref,
            send_sem=up_send,
            recv_sem=up_recv,
            device_id={"gx": me + 1},
            device_id_type=MESH,
        )

    each_holder(
        lambda which, holder: to_holder(which, holder).start(),
        lambda holder: to_self(holder).start(),
    )

    @pl.when(me > 0)
    def _():
        to_below(0, ef).start()
        to_below(1, ea).start()

    for load in loads:
        load.wait()
    for r in range(2):
        ex, ey, ez = eb[r, 0], eb[r, 1], eb[r, 2]
        part[r, 0] = hb[r, 0] - DT * (ahead(ez, 1) - ez + ey)
        part[r, 1] = hb[r, 1] + DT * (ex + (ahead(ez, 0) - ez))

    @pl.when(me < n - 1)
    def _():
        to_above().start()

    each_holder(
        lambda which, holder: to_holder(which, holder).wait_send(),
        lambda holder: to_self(holder).wait(),
    )

    @pl.when(me > 0)
    def _():
        to_below(0, ef).wait_send()
        to_below(1, ea).wait_send()
        to_above().wait_recv()

    @pl.when(me < n - 1)
    def _():
        to_above().wait_send()
        to_below(0, ef).wait_recv()
        to_below(1, ea).wait_recv()

    base, low, high = slot_range(me, n, depth)

    @pl.loop(low, high)
    def _(owner):
        @pl.when(owner != me)
        def _():
            pltpu.make_async_remote_copy(
                src_ref=rho,
                dst_ref=slots_ref.at[owner - base],
                send_sem=send_sem.at[0],
                recv_sem=slot_recv.at[owner - base],
                device_id={"gx": owner},
                device_id_type=MESH,
            ).wait_recv()


def step_kernel(
    n,
    start_ref,
    amp_ref,
    source_ref,
    monitor_ref,
    ef_in,
    hf_in,
    pf_in,
    jf_in,
    ea_in,
    ha_in,
    pa_in,
    ja_in,
    below_in,
    above_in,
    slots_in,
    ef_out,
    hf_out,
    ea_out,
    ha_out,
    product_out,
    e,
    h,
    p,
    j,
    below,
    above,
    rho,
    drive,
    seen,
    product,
    en,
    hn,
    in_sem,
    out_sem,
    side_sem,
):
    me = lax.axis_index("gx")
    _, _, depth, nx, ny = e.shape
    start = start_ref[0]
    first_slot = 2 * depth - 1 - start
    sides = [
        pltpu.make_async_copy(below_in, below, side_sem.at[0]),
        pltpu.make_async_copy(slots_in.at[pl.ds(first_slot, depth)], rho, side_sem.at[1]),
        pltpu.make_async_copy(above_in, above, side_sem.at[2]),
    ]
    loads = {}
    pairs = ((e, ef_in, ea_in), (h, hf_in, ha_in), (j, jf_in, ja_in), (p, pf_in, pa_in))
    for l in range(depth):
        for k, (ref, *sources) in enumerate(pairs):
            for r, source in enumerate(sources):
                loads[k, l, r] = pltpu.make_async_copy(
                    source.at[:, l], ref.at[r, :, l], in_sem.at[k, l, r]
                )
    for r in range(2):
        loads[0, 0, r].start()
    for l in range(depth):
        for r in range(2):
            if l + 1 < depth:
                loads[0, l + 1, r].start()
            for k in (1, 2, 3):
                loads[k, l, r].start()
        if l == 0:
            sides[0].start()
            sides[1].start()
    sides[2].start()

    drive[...] = jnp.zeros_like(drive)
    seen[...] = jnp.zeros_like(seen)
    first_row = me * (depth * nx)
    lanes = lax.broadcasted_iota(jnp.int32, (1, ny), 1)

    @pl.loop(0, source_ref.shape[0])
    def _(s):
        cell = source_ref[s]
        row = cell // ny - first_row

        @pl.when((row >= 0) & (row < depth * nx))
        def _():
            hit = lanes == cell % ny
            for c in range(3):
                drive[c, pl.ds(row, 1), :] += jnp.where(hit, amp_ref[c, s], 0.0)

    @pl.loop(0, monitor_ref.shape[0])
    def _(s):
        cell = monitor_ref[s]
        row = cell // ny - first_row

        @pl.when((row >= 0) & (row < depth * nx))
        def _():
            seen[pl.ds(row, 1), :] += jnp.where(lanes == cell % ny, 1.0, 0.0)

    stores = []

    def store(source, dst, *index):
        copy = pltpu.make_async_copy(source, dst, out_sem.at[*index])
        copy.start()
        stores.append(copy)

    for r in range(2):
        loads[0, 0, r].wait()
    for l in range(depth):
        for r in range(2):
            if l + 1 < depth:
                loads[0, l + 1, r].wait()
            for k in (1, 2, 3):
                loads[k, l, r].wait()
        if l == 0:
            sides[0].wait()
            sides[1].wait()
        if l == depth - 1:
            sides[2].wait()
        owner = me * depth + l - start
        density = jnp.where((owner >= 0) & (owner < n), rho[l], 0.0)
        scale = DT / (1.0 + EPS_RANGE * density)
        strength = STRENGTH_BASE + STRENGTH_RANGE * density
        rows = pl.ds(l * nx, nx)
        old = new = None
        for r in range(2):
            ex, ey, ez = e[r, 0, l], e[r, 1, l], e[r, 2, l]
            if l + 1 < depth:
                ex_up, ey_up = e[r, 0, l + 1], e[r, 1, l + 1]
            else:
                ex_up = jnp.where(me < n - 1, above[r, 0], 0.0)
                ey_up = jnp.where(me < n - 1, above[r, 1], 0.0)
            hx = h[r, 0, l] - DT * ((ahead(ez, 1) - ez) - (ey_up - ey))
            hy = h[r, 1, l] - DT * ((ex_up - ex) - (ahead(ez, 0) - ez))
            hz = h[r, 2, l] - DT * ((ahead(ey, 0) - ey) - (ahead(ex, 1) - ex))
            hn[r, 0, l] = hx
            hn[r, 1, l] = hy
            hn[r, 2, l] = hz
            store(hn.at[r, :, l], (hf_out, ha_out)[r].at[:, l], 1, l, r)
            if l:
                hx_low, hy_low = hn[r, 0, l - 1], hn[r, 1, l - 1]
            else:
                hx_low = jnp.where(me > 0, below[r, 0] + DT * ey, 0.0)
                hy_low = jnp.where(me > 0, below[r, 1] - DT * ex, 0.0)
            curl = (
                (hz - behind(hz, 1)) - (hy - hy_low),
                (hx - hx_low) - (hz - behind(hz, 0)),
                (hy - behind(hy, 0)) - (hx - behind(hx, 1)),
            )
            fields = (ex, ey, ez)
            result = []
            for c in range(3):
                push = drive[c, rows, :] if r == 0 else seen[rows, :] * e[0, c, l]
                current = (
                    (1.0 - DAMPING * DT / 2.0) * j[r, c, l]
                    + DT * (strength * fields[c] - p[r, c, l])
                ) * (1.0 / (1.0 + DAMPING * DT / 2.0))
                result.append(fields[c] + scale * (curl[c] - current + push))
                en[r, c, l] = result[c]
            store(en.at[r, :, l], (ef_out, ea_out)[r].at[:, l], 0, l, r)
            if r == 0:
                old, new = fields, result
            else:
                product[l] = sum(
                    result[c] * ((new[c] - old[c]) + GAIN_FIELD * new[c]) for c in range(3)
                )
    last = pltpu.make_async_copy(
        product, product_out.at[pl.ds(first_slot, depth)], side_sem.at[3]
    )
    last.start()
    for copy in stores:
        copy.wait()
    last.wait()


def gradient_kernel(
    n,
    depth,
    radius_ref,
    start_ref,
    product_ref,
    grad_ref,
    arrived,
    send_sem,
    recv_sem,
    self_sem,
):
    me = lax.axis_index("gx")
    first, second, shift = holders(me, depth)
    base, low, high = slot_range(me, n, depth)
    barrier = pltpu.get_barrier_semaphore()
    for holder, used in ((first, shift >= 0), (second, shift != 0)):

        @pl.when(used & (holder != me))
        def _():
            pl.semaphore_signal(barrier, inc=1, device_id={"gx": holder}, device_id_type=MESH)

    inside = jnp.where((me >= low) & (me < high), 1, 0)
    count = jnp.maximum(high - low, 0) - inside

    @pl.when(count > 0)
    def _():
        pl.semaphore_wait(barrier, count)

    def back(owner):
        slot = owner - base
        which = jnp.where(slot >= depth - 1, 0, 1)
        return pltpu.make_async_remote_copy(
            src_ref=product_ref.at[slot],
            dst_ref=arrived.at[which],
            send_sem=send_sem.at[slot],
            recv_sem=recv_sem.at[which],
            device_id={"gx": owner},
            device_id_type=MESH,
        )

    def keep():
        slot = me - base
        which = jnp.where(slot >= depth - 1, 0, 1)
        return pltpu.make_async_copy(product_ref.at[slot], arrived.at[which], self_sem)

    @pl.loop(low, high)
    def _(owner):
        pl.when(owner != me)(lambda: back(owner).start())
        pl.when(owner == me)(lambda: keep().start())

    for which, holder, used in ((0, first, shift >= 0), (1, second, shift != 0)):

        @pl.when(used & (holder != me))
        def _():
            pltpu.make_async_remote_copy(
                src_ref=product_ref.at[0],
                dst_ref=arrived.at[which],
                send_sem=send_sem.at[0],
                recv_sem=recv_sem.at[which],
                device_id={"gx": holder},
                device_id_type=MESH,
            ).wait_recv()

        pl.when(used & (holder == me))(lambda: keep().wait())

    radius = radius_ref[0]
    in_first = start_ref[0] + me < (first + 1) * depth
    plane = jnp.where(in_first, arrived[0], arrived[1])
    grad_ref[0] = band_product(plane * inverse_sums(plane.shape, radius), radius)

    @pl.loop(low, high)
    def _(owner):
        pl.when(owner != me)(lambda: back(owner).wait_send())


def body(
    n,
    e_forward,
    h_forward,
    p_forward,
    j_forward,
    e_adjoint,
    h_adjoint,
    p_adjoint,
    j_adjoint,
    design,
    source_amp,
    source_cell,
    monitor_cell,
    slab_start,
    radius,
):
    _, depth, nx, ny = e_forward.shape
    slots = 2 * depth - 1
    dma = pltpu.SemaphoreType.DMA
    below, above, densities = pl.pallas_call(
        functools.partial(exchange_kernel, n),
        out_shape=(
            jax.ShapeDtypeStruct((2, 2, nx, ny), F32),
            jax.ShapeDtypeStruct((2, 2, nx, ny), F32),
            jax.ShapeDtypeStruct((slots, nx, ny), F32),
        ),
        in_specs=[SMEM, VMEM, ANY, ANY, ANY, ANY],
        out_specs=(ANY, ANY, ANY),
        scratch_shapes=[
            pltpu.VMEM((2, 3, nx, ny), F32),
            pltpu.VMEM((2, 2, nx, ny), F32),
            pltpu.VMEM((2, 2, nx, ny), F32),
            pltpu.VMEM((nx, ny), F32),
            dma((2, 2)),
            dma((2,)),
            dma(()),
            dma(()),
            dma((2,)),
            dma((2,)),
            dma((slots,)),
            dma(()),
        ],
        compiler_params=pltpu.CompilerParams(
            collective_id=0, has_side_effects=True, vmem_limit_bytes=6 * 1024 * 1024
        ),
        name="exchange",
    )(radius, design, e_forward, e_adjoint, h_forward, h_adjoint)
    field = jax.ShapeDtypeStruct(e_forward.shape, F32)
    both = pltpu.VMEM((2,) + e_forward.shape, F32)
    ef, hf, ea, ha, product = pl.pallas_call(
        functools.partial(step_kernel, n),
        out_shape=(field, field, field, field, jax.ShapeDtypeStruct((slots, nx, ny), F32)),
        in_specs=[SMEM] * 4 + [ANY] * 11,
        out_specs=(ANY,) * 5,
        scratch_shapes=[
            both,
            both,
            both,
            both,
            pltpu.VMEM((2, 2, nx, ny), F32),
            pltpu.VMEM((2, 2, nx, ny), F32),
            pltpu.VMEM((depth, nx, ny), F32),
            pltpu.VMEM((3, depth * nx, ny), F32),
            pltpu.VMEM((depth * nx, ny), F32),
            pltpu.VMEM((depth, nx, ny), F32),
            both,
            both,
            dma((4, depth, 2)),
            dma((2, depth, 2)),
            dma((4,)),
        ],
        compiler_params=pltpu.CompilerParams(vmem_limit_bytes=24 * 1024 * 1024),
        name="step",
    )(
        slab_start,
        source_amp.T,
        source_cell,
        monitor_cell,
        e_forward,
        h_forward,
        p_forward,
        j_forward,
        e_adjoint,
        h_adjoint,
        p_adjoint,
        j_adjoint,
        below,
        above,
        densities,
    )
    grad = pl.pallas_call(
        functools.partial(gradient_kernel, n, depth),
        out_shape=jax.ShapeDtypeStruct(design.shape, F32),
        in_specs=[SMEM, SMEM, ANY],
        out_specs=VMEM,
        scratch_shapes=[
            pltpu.VMEM((2, nx, ny), F32),
            dma((slots,)),
            dma((2,)),
            dma(()),
        ],
        compiler_params=pltpu.CompilerParams(
            collective_id=1, has_side_effects=True, vmem_limit_bytes=6 * 1024 * 1024
        ),
        name="gradient",
    )(radius, slab_start, product)
    return ef, hf, ea, ha, grad


def solution(mesh):
    field = P(None, ("grp", "gx"), None, None)
    plane = P(("grp", "gx"), None, None)
    return jax.shard_map(
        functools.partial(body, mesh.shape["gx"]),
        mesh=mesh,
        in_specs=(field,) * 8 + (plane, P("grp", None)) + (P("grp"),) * 4,
        out_specs=(field,) * 4 + (plane,),
        check_vma=False,
    )
```

```python
import functools

import jax
import jax.numpy as jnp
from jax import lax
from jax.experimental import pallas as pl
from jax.experimental.pallas import tpu as pltpu
from jax.sharding import PartitionSpec as P

DT = 0.5
EPS_RANGE = 10.0
STRENGTH_BASE = 0.5
STRENGTH_RANGE = 3.0
DAMPING = 0.2
GAIN_FIELD = 0.25
BIG = 60 * 1024 * 1024
MESH = pl.DeviceIdType.MESH
F32 = jnp.float32
BF16 = jnp.bfloat16
HBM = pl.BlockSpec(memory_space=pltpu.HBM)
SMEM = pl.BlockSpec(memory_space=pltpu.SMEM)
VMEM = pl.BlockSpec(memory_space=pltpu.VMEM)


def slot_range(me, n, depth):
    base = depth * (me - 1) - (depth - 1)
    return base, jnp.maximum(base, 0), jnp.minimum(base + 2 * depth - 1, n)


def holders(me, depth):
    first = me // depth + 1
    return first, first + 1, me % depth


def ahead(v, axis):
    size = v.shape[axis]
    pos = lax.broadcasted_iota(jnp.int32, v.shape, axis)
    return jnp.where(pos == size - 1, 0.0, pltpu.roll(v, size - 1, axis))


def behind(v, axis):
    pos = lax.broadcasted_iota(jnp.int32, v.shape, axis)
    return jnp.where(pos == 0, 0.0, pltpu.roll(v, 1, axis))


def triangle(size, radius):
    a = lax.broadcasted_iota(jnp.int32, (size, size), 0)
    b = lax.broadcasted_iota(jnp.int32, (size, size), 1)
    return jnp.maximum(radius + 1 - jnp.abs(a - b), 0).astype(F32).astype(BF16)


def row_sums(shape, axis, radius):
    pos = lax.broadcasted_iota(jnp.int32, shape, axis)
    low = jnp.maximum(radius - pos, 0)
    high = jnp.maximum(radius - (shape[axis] - 1 - pos), 0)
    whole = (radius + 1) * (radius + 1)
    low, high = low.astype(F32), high.astype(F32)
    return whole.astype(F32) - 0.5 * (low * (low + 1.0) + high * (high + 1.0))


def halves(v):
    big = v.astype(BF16)
    return big, (v - big.astype(F32)).astype(BF16)


def band_product(plane, radius):
    nx, ny = plane.shape
    tx, ty = triangle(nx, radius), triangle(ny, radius)
    big, small = halves(plane)
    both = jnp.dot(jnp.concatenate([big, small], 0), ty, preferred_element_type=F32)
    big, small = halves(both[:nx] + both[nx:])
    return jnp.dot(tx, big, preferred_element_type=F32) + jnp.dot(
        tx, small, preferred_element_type=F32
    )


def inverse_sums(shape, radius):
    return 1.0 / (row_sums(shape, 0, radius) * row_sums(shape, 1, radius))


def exchange_kernel(
    n,
    radius_ref,
    design_ref,
    ef,
    ea,
    hf,
    ha,
    below_ref,
    above_ref,
    slots_ref,
    eb,
    hb,
    part,
    rho,
    load_sem,
    send_sem,
    up_send,
    up_recv,
    down_send,
    down_recv,
    slot_recv,
    self_sem,
):
    me = lax.axis_index("gx")
    depth = ef.shape[1]
    loads = []
    for r, (e, h) in enumerate(((ef, hf), (ea, ha))):
        loads.append(pltpu.make_async_copy(e.at[:, depth - 1], eb.at[r], load_sem.at[r, 0]))
        loads.append(pltpu.make_async_copy(h.at[0:2, depth - 1], hb.at[r], load_sem.at[r, 1]))
    for load in loads:
        load.start()

    barrier = pltpu.get_barrier_semaphore()

    @pl.loop(1, n)
    def _(k):
        pl.semaphore_signal(
            barrier, inc=1, device_id={"gx": lax.rem(me + k, n)}, device_id_type=MESH
        )

    radius = radius_ref[0]
    plane = design_ref[0]
    rho[...] = band_product(plane, radius) * inverse_sums(plane.shape, radius)
    pl.semaphore_wait(barrier, n - 1)

    first, second, shift = holders(me, depth)

    def to_holder(which, holder):
        slot = me - (depth * (holder - 1) - (depth - 1))
        return pltpu.make_async_remote_copy(
            src_ref=rho,
            dst_ref=slots_ref.at[slot],
            send_sem=send_sem.at[which],
            recv_sem=slot_recv.at[slot],
            device_id={"gx": holder},
            device_id_type=MESH,
        )

    def to_self(holder):
        slot = me - (depth * (holder - 1) - (depth - 1))
        return pltpu.make_async_copy(rho, slots_ref.at[slot], self_sem)

    def each_holder(remote, local):
        for which, holder, used in ((0, first, shift >= 0), (1, second, shift != 0)):
            pl.when(used & (holder != me))(functools.partial(remote, which, holder))
            pl.when(used & (holder == me))(functools.partial(local, holder))

    def to_below(r, e):
        return pltpu.make_async_remote_copy(
            src_ref=e.at[0:2, 0],
            dst_ref=above_ref.at[r],
            send_sem=down_send.at[r],
            recv_sem=down_recv.at[r],
            device_id={"gx": me - 1},
            device_id_type=MESH,
        )

    def to_above():
        return pltpu.make_async_remote_copy(
            src_ref=part,
            dst_ref=below_ref,
            send_sem=up_send,
            recv_sem=up_recv,
            device_id={"gx": me + 1},
            device_id_type=MESH,
        )

    each_holder(
        lambda which, holder: to_holder(which, holder).start(),
        lambda holder: to_self(holder).start(),
    )

    @pl.when(me > 0)
    def _():
        to_below(0, ef).start()
        to_below(1, ea).start()

    for load in loads:
        load.wait()
    for r in range(2):
        ex, ey, ez = eb[r, 0], eb[r, 1], eb[r, 2]
        part[r, 0] = hb[r, 0] - DT * (ahead(ez, 1) - ez + ey)
        part[r, 1] = hb[r, 1] + DT * (ex + (ahead(ez, 0) - ez))

    @pl.when(me < n - 1)
    def _():
        to_above().start()

    each_holder(
        lambda which, holder: to_holder(which, holder).wait_send(),
        lambda holder: to_self(holder).wait(),
    )

    @pl.when(me > 0)
    def _():
        to_below(0, ef).wait_send()
        to_below(1, ea).wait_send()
        to_above().wait_recv()

    @pl.when(me < n - 1)
    def _():
        to_above().wait_send()
        to_below(0, ef).wait_recv()
        to_below(1, ea).wait_recv()

    base, low, high = slot_range(me, n, depth)

    @pl.loop(low, high)
    def _(owner):
        @pl.when(owner != me)
        def _():
            pltpu.make_async_remote_copy(
                src_ref=rho,
                dst_ref=slots_ref.at[owner - base],
                send_sem=send_sem.at[0],
                recv_sem=slot_recv.at[owner - base],
                device_id={"gx": owner},
                device_id_type=MESH,
            ).wait_recv()


def step_kernel(
    n,
    start_ref,
    amp_ref,
    source_ref,
    monitor_ref,
    ef_in,
    hf_in,
    pf_in,
    jf_in,
    ea_in,
    ha_in,
    pa_in,
    ja_in,
    below_in,
    above_in,
    slots_in,
    ef_out,
    hf_out,
    ea_out,
    ha_out,
    product_out,
    e,
    h,
    p,
    j,
    below,
    above,
    rho,
    drive,
    seen,
    product,
    en,
    hn,
    in_sem,
    out_sem,
    side_sem,
):
    me = lax.axis_index("gx")
    _, _, depth, nx, ny = e.shape
    start = start_ref[0]
    first_slot = 2 * depth - 1 - start
    sides = [
        pltpu.make_async_copy(below_in, below, side_sem.at[0]),
        pltpu.make_async_copy(slots_in.at[pl.ds(first_slot, depth)], rho, side_sem.at[1]),
        pltpu.make_async_copy(above_in, above, side_sem.at[2]),
    ]
    loads = {}
    pairs = ((e, ef_in, ea_in), (h, hf_in, ha_in), (j, jf_in, ja_in), (p, pf_in, pa_in))
    for l in range(depth):
        for k, (ref, *sources) in enumerate(pairs):
            for r, source in enumerate(sources):
                loads[k, l, r] = pltpu.make_async_copy(
                    source.at[:, l], ref.at[r, :, l], in_sem.at[k, l, r]
                )
    for r in range(2):
        loads[0, 0, r].start()
    for l in range(depth):
        for r in range(2):
            if l + 1 < depth:
                loads[0, l + 1, r].start()
            for k in (1, 2, 3):
                loads[k, l, r].start()
        if l == 0:
            sides[0].start()
            sides[1].start()
    sides[2].start()

    drive[...] = jnp.zeros_like(drive)
    seen[...] = jnp.zeros_like(seen)
    first_row = me * (depth * nx)
    lanes = lax.broadcasted_iota(jnp.int32, (1, ny), 1)

    @pl.loop(0, source_ref.shape[0])
    def _(s):
        cell = source_ref[s]
        row = cell // ny - first_row

        @pl.when((row >= 0) & (row < depth * nx))
        def _():
            hit = lanes == cell % ny
            for c in range(3):
                drive[c, pl.ds(row, 1), :] += jnp.where(hit, amp_ref[c, s], 0.0)

    @pl.loop(0, monitor_ref.shape[0])
    def _(s):
        cell = monitor_ref[s]
        row = cell // ny - first_row

        @pl.when((row >= 0) & (row < depth * nx))
        def _():
            seen[pl.ds(row, 1), :] += jnp.where(lanes == cell % ny, 1.0, 0.0)

    stores = []

    def store(source, dst, *index):
        copy = pltpu.make_async_copy(source, dst, out_sem.at[*index])
        copy.start()
        stores.append(copy)

    for r in range(2):
        loads[0, 0, r].wait()
    for l in range(depth):
        for r in range(2):
            if l + 1 < depth:
                loads[0, l + 1, r].wait()
            for k in (1, 2, 3):
                loads[k, l, r].wait()
        if l == 0:
            sides[0].wait()
            sides[1].wait()
        if l == depth - 1:
            sides[2].wait()
        owner = me * depth + l - start
        density = jnp.where((owner >= 0) & (owner < n), rho[l], 0.0)
        scale = DT / (1.0 + EPS_RANGE * density)
        strength = STRENGTH_BASE + STRENGTH_RANGE * density
        rows = pl.ds(l * nx, nx)
        old = new = None
        for r in range(2):
            ex, ey, ez = e[r, 0, l], e[r, 1, l], e[r, 2, l]
            if l + 1 < depth:
                ex_up, ey_up = e[r, 0, l + 1], e[r, 1, l + 1]
            else:
                ex_up = jnp.where(me < n - 1, above[r, 0], 0.0)
                ey_up = jnp.where(me < n - 1, above[r, 1], 0.0)
            hx = h[r, 0, l] - DT * ((ahead(ez, 1) - ez) - (ey_up - ey))
            hy = h[r, 1, l] - DT * ((ex_up - ex) - (ahead(ez, 0) - ez))
            hz = h[r, 2, l] - DT * ((ahead(ey, 0) - ey) - (ahead(ex, 1) - ex))
            hn[r, 0, l] = hx
            hn[r, 1, l] = hy
            hn[r, 2, l] = hz
            store(hn.at[r, :, l], (hf_out, ha_out)[r].at[:, l], 1, l, r)
            if l:
                hx_low, hy_low = hn[r, 0, l - 1], hn[r, 1, l - 1]
            else:
                hx_low = jnp.where(me > 0, below[r, 0] + DT * ey, 0.0)
                hy_low = jnp.where(me > 0, below[r, 1] - DT * ex, 0.0)
            curl = (
                (hz - behind(hz, 1)) - (hy - hy_low),
                (hx - hx_low) - (hz - behind(hz, 0)),
                (hy - behind(hy, 0)) - (hx - behind(hx, 1)),
            )
            fields = (ex, ey, ez)
            result = []
            for c in range(3):
                push = drive[c, rows, :] if r == 0 else seen[rows, :] * e[0, c, l]
                current = (
                    (1.0 - DAMPING * DT / 2.0) * j[r, c, l]
                    + DT * (strength * fields[c] - p[r, c, l])
                ) * (1.0 / (1.0 + DAMPING * DT / 2.0))
                result.append(fields[c] + scale * (curl[c] - current + push))
                en[r, c, l] = result[c]
            store(en.at[r, :, l], (ef_out, ea_out)[r].at[:, l], 0, l, r)
            if r == 0:
                old, new = fields, result
            else:
                product[l] = sum(
                    result[c] * ((new[c] - old[c]) + GAIN_FIELD * new[c]) for c in range(3)
                )
    last = pltpu.make_async_copy(
        product, product_out.at[pl.ds(first_slot, depth)], side_sem.at[3]
    )
    last.start()
    for copy in stores:
        copy.wait()
    last.wait()


def gradient_kernel(
    n,
    depth,
    radius_ref,
    start_ref,
    product_ref,
    grad_ref,
    arrived,
    send_sem,
    recv_sem,
    self_sem,
):
    me = lax.axis_index("gx")
    first, second, shift = holders(me, depth)
    base, low, high = slot_range(me, n, depth)
    barrier = pltpu.get_barrier_semaphore()
    for holder, used in ((first, shift >= 0), (second, shift != 0)):

        @pl.when(used & (holder != me))
        def _():
            pl.semaphore_signal(barrier, inc=1, device_id={"gx": holder}, device_id_type=MESH)

    inside = jnp.where((me >= low) & (me < high), 1, 0)
    count = jnp.maximum(high - low, 0) - inside

    @pl.when(count > 0)
    def _():
        pl.semaphore_wait(barrier, count)

    def back(owner):
        slot = owner - base
        which = jnp.where(slot >= depth - 1, 0, 1)
        return pltpu.make_async_remote_copy(
            src_ref=product_ref.at[slot],
            dst_ref=arrived.at[which],
            send_sem=send_sem.at[slot],
            recv_sem=recv_sem.at[which],
            device_id={"gx": owner},
            device_id_type=MESH,
        )

    def keep():
        slot = me - base
        which = jnp.where(slot >= depth - 1, 0, 1)
        return pltpu.make_async_copy(product_ref.at[slot], arrived.at[which], self_sem)

    @pl.loop(low, high)
    def _(owner):
        pl.when(owner != me)(lambda: back(owner).start())
        pl.when(owner == me)(lambda: keep().start())

    for which, holder, used in ((0, first, shift >= 0), (1, second, shift != 0)):

        @pl.when(used & (holder != me))
        def _():
            pltpu.make_async_remote_copy(
                src_ref=product_ref.at[0],
                dst_ref=arrived.at[which],
                send_sem=send_sem.at[0],
                recv_sem=recv_sem.at[which],
                device_id={"gx": holder},
                device_id_type=MESH,
            ).wait_recv()

        pl.when(used & (holder == me))(lambda: keep().wait())

    radius = radius_ref[0]
    in_first = start_ref[0] + me < (first + 1) * depth
    plane = jnp.where(in_first, arrived[0], arrived[1])
    grad_ref[0] = band_product(plane * inverse_sums(plane.shape, radius), radius)

    @pl.loop(low, high)
    def _(owner):
        pl.when(owner != me)(lambda: back(owner).wait_send())


def body(
    n,
    e_forward,
    h_forward,
    p_forward,
    j_forward,
    e_adjoint,
    h_adjoint,
    p_adjoint,
    j_adjoint,
    design,
    source_amp,
    source_cell,
    monitor_cell,
    slab_start,
    radius,
):
    _, depth, nx, ny = e_forward.shape
    slots = 2 * depth - 1
    dma = pltpu.SemaphoreType.DMA
    below, above, densities = pl.pallas_call(
        functools.partial(exchange_kernel, n),
        out_shape=(
            jax.ShapeDtypeStruct((2, 2, nx, ny), F32),
            jax.ShapeDtypeStruct((2, 2, nx, ny), F32),
            jax.ShapeDtypeStruct((slots, nx, ny), F32),
        ),
        in_specs=[SMEM, VMEM, HBM, HBM, HBM, HBM],
        out_specs=(HBM, HBM, HBM),
        scratch_shapes=[
            pltpu.VMEM((2, 3, nx, ny), F32),
            pltpu.VMEM((2, 2, nx, ny), F32),
            pltpu.VMEM((2, 2, nx, ny), F32),
            pltpu.VMEM((nx, ny), F32),
            dma((2, 2)),
            dma((2,)),
            dma(()),
            dma(()),
            dma((2,)),
            dma((2,)),
            dma((slots,)),
            dma(()),
        ],
        compiler_params=pltpu.CompilerParams(
            collective_id=0, has_side_effects=True, vmem_limit_bytes=BIG
        ),
        name="exchange",
    )(radius, design, e_forward, e_adjoint, h_forward, h_adjoint)
    field = jax.ShapeDtypeStruct(e_forward.shape, F32)
    both = pltpu.VMEM((2,) + e_forward.shape, F32)
    ef, hf, ea, ha, product = pl.pallas_call(
        functools.partial(step_kernel, n),
        out_shape=(field, field, field, field, jax.ShapeDtypeStruct((slots, nx, ny), F32)),
        in_specs=[SMEM] * 4 + [HBM] * 11,
        out_specs=(HBM,) * 5,
        scratch_shapes=[
            both,
            both,
            both,
            both,
            pltpu.VMEM((2, 2, nx, ny), F32),
            pltpu.VMEM((2, 2, nx, ny), F32),
            pltpu.VMEM((depth, nx, ny), F32),
            pltpu.VMEM((3, depth * nx, ny), F32),
            pltpu.VMEM((depth * nx, ny), F32),
            pltpu.VMEM((depth, nx, ny), F32),
            both,
            both,
            dma((4, depth, 2)),
            dma((2, depth, 2)),
            dma((4,)),
        ],
        compiler_params=pltpu.CompilerParams(vmem_limit_bytes=BIG),
        name="step",
    )(
        slab_start,
        source_amp.T,
        source_cell,
        monitor_cell,
        e_forward,
        h_forward,
        p_forward,
        j_forward,
        e_adjoint,
        h_adjoint,
        p_adjoint,
        j_adjoint,
        below,
        above,
        densities,
    )
    grad = pl.pallas_call(
        functools.partial(gradient_kernel, n, depth),
        out_shape=jax.ShapeDtypeStruct(design.shape, F32),
        in_specs=[SMEM, SMEM, HBM],
        out_specs=VMEM,
        scratch_shapes=[
            pltpu.VMEM((2, nx, ny), F32),
            dma((slots,)),
            dma((2,)),
            dma(()),
        ],
        compiler_params=pltpu.CompilerParams(
            collective_id=1, has_side_effects=True, vmem_limit_bytes=BIG
        ),
        name="gradient",
    )(radius, slab_start, product)
    return ef, hf, ea, ha, grad


def solution(mesh):
    field = P(None, ("grp", "gx"), None, None)
    plane = P(("grp", "gx"), None, None)
    return jax.shard_map(
        functools.partial(body, mesh.shape["gx"]),
        mesh=mesh,
        in_specs=(field,) * 8 + (plane, P("grp", None)) + (P("grp"),) * 4,
        out_specs=(field,) * 4 + (plane,),
        check_vma=False,
    )
```

```python
import functools

import jax
import jax.numpy as jnp
from jax import lax
from jax.experimental import pallas as pl
from jax.experimental.pallas import tpu as pltpu
from jax.sharding import PartitionSpec as P

DT = 0.5
EPS_RANGE = 10.0
STRENGTH_BASE = 0.5
STRENGTH_RANGE = 3.0
DAMPING = 0.2
GAIN_FIELD = 0.25
BIG = 60 * 1024 * 1024
MESH = pl.DeviceIdType.MESH
F32 = jnp.float32
BF16 = jnp.bfloat16
HBM = pl.BlockSpec(memory_space=pltpu.HBM)
SMEM = pl.BlockSpec(memory_space=pltpu.SMEM)
VMEM = pl.BlockSpec(memory_space=pltpu.VMEM)


def ahead(v, axis):
    size = v.shape[axis]
    pos = lax.broadcasted_iota(jnp.int32, v.shape, axis)
    return jnp.where(pos == size - 1, 0.0, pltpu.roll(v, size - 1, axis))


def behind(v, axis):
    pos = lax.broadcasted_iota(jnp.int32, v.shape, axis)
    return jnp.where(pos == 0, 0.0, pltpu.roll(v, 1, axis))


def triangle(size, radius):
    a = lax.broadcasted_iota(jnp.int32, (size, size), 0)
    b = lax.broadcasted_iota(jnp.int32, (size, size), 1)
    return jnp.maximum(radius + 1 - jnp.abs(a - b), 0).astype(F32).astype(BF16)


def row_sums(shape, axis, radius):
    pos = lax.broadcasted_iota(jnp.int32, shape, axis)
    low = jnp.maximum(radius - pos, 0)
    high = jnp.maximum(radius - (shape[axis] - 1 - pos), 0)
    whole = (radius + 1) * (radius + 1)
    low, high = low.astype(F32), high.astype(F32)
    return whole.astype(F32) - 0.5 * (low * (low + 1.0) + high * (high + 1.0))


def halves(v):
    big = v.astype(BF16)
    return big, (v - big.astype(F32)).astype(BF16)


def band_product(plane, radius):
    nx, ny = plane.shape
    tx, ty = triangle(nx, radius), triangle(ny, radius)
    big, small = halves(plane)
    both = jnp.dot(jnp.concatenate([big, small], 0), ty, preferred_element_type=F32)
    big, small = halves(both[:nx] + both[nx:])
    return jnp.dot(tx, big, preferred_element_type=F32) + jnp.dot(
        tx, small, preferred_element_type=F32
    )


def inverse_sums(shape, radius):
    return 1.0 / (row_sums(shape, 0, radius) * row_sums(shape, 1, radius))


def exchange_kernel(
    n,
    radius_ref,
    design_ref,
    ef,
    ea,
    hf,
    ha,
    below_ref,
    above_ref,
    slots_ref,
    eb,
    hb,
    part,
    rho,
    load_sem,
    send_sem,
    onward_send,
    up_send,
    up_recv,
    down_send,
    down_recv,
    slot_recv,
    self_sem,
):
    me = lax.axis_index("gx")
    depth = ef.shape[1]
    loads = []
    for r, (e, h) in enumerate(((ef, hf), (ea, ha))):
        loads.append(pltpu.make_async_copy(e.at[:, depth - 1], eb.at[r], load_sem.at[r, 0]))
        loads.append(pltpu.make_async_copy(h.at[0:2, depth - 1], hb.at[r], load_sem.at[r, 1]))
    for load in loads:
        load.start()

    barrier = pltpu.get_barrier_semaphore()

    @pl.loop(1, n)
    def _(k):
        pl.semaphore_signal(
            barrier, inc=1, device_id={"gx": lax.rem(me + k, n)}, device_id_type=MESH
        )

    radius = radius_ref[0]
    plane = design_ref[0]
    rho[...] = band_product(plane, radius) * inverse_sums(plane.shape, radius)
    pl.semaphore_wait(barrier, n - 1)

    first = me // depth + 1

    def to_holder():
        slot = me % depth + depth - 1
        return pltpu.make_async_remote_copy(
            src_ref=rho,
            dst_ref=slots_ref.at[slot],
            send_sem=send_sem,
            recv_sem=slot_recv.at[slot],
            device_id={"gx": first},
            device_id_type=MESH,
        )

    def to_self():
        return pltpu.make_async_copy(rho, slots_ref.at[me % depth + depth - 1], self_sem)

    def onward(k):
        return pltpu.make_async_remote_copy(
            src_ref=slots_ref.at[depth - 1 + k],
            dst_ref=slots_ref.at[k - 1],
            send_sem=onward_send.at[k],
            recv_sem=slot_recv.at[k - 1],
            device_id={"gx": me + 1},
            device_id_type=MESH,
        )

    def landed(slot):
        return pltpu.make_async_remote_copy(
            src_ref=rho,
            dst_ref=slots_ref.at[slot],
            send_sem=send_sem,
            recv_sem=slot_recv.at[slot],
            device_id={"gx": first},
            device_id_type=MESH,
        )

    def to_below(r, e):
        return pltpu.make_async_remote_copy(
            src_ref=e.at[0:2, 0],
            dst_ref=above_ref.at[r],
            send_sem=down_send.at[r],
            recv_sem=down_recv.at[r],
            device_id={"gx": me - 1},
            device_id_type=MESH,
        )

    def to_above():
        return pltpu.make_async_remote_copy(
            src_ref=part,
            dst_ref=below_ref,
            send_sem=up_send,
            recv_sem=up_recv,
            device_id={"gx": me + 1},
            device_id_type=MESH,
        )

    pl.when(first != me)(lambda: to_holder().start())
    pl.when(first == me)(lambda: to_self().start())

    @pl.when(me > 0)
    def _():
        to_below(0, ef).start()
        to_below(1, ea).start()

    for load in loads:
        load.wait()
    for r in range(2):
        ex, ey, ez = eb[r, 0], eb[r, 1], eb[r, 2]
        part[r, 0] = hb[r, 0] - DT * (ahead(ez, 1) - ez + ey)
        part[r, 1] = hb[r, 1] + DT * (ex + (ahead(ez, 0) - ez))

    @pl.when(me < n - 1)
    def _():
        to_above().start()

    @pl.when((me >= 1) & (depth * (me - 1) < n))
    def _():
        @pl.loop(0, depth)
        def _(k):
            owner = depth * (me - 1) + k
            pl.when((owner < n) & (owner != me))(lambda: landed(depth - 1 + k).wait_recv())
            pl.when(owner == me)(lambda: to_self().wait())
            pl.when((owner < n) & (k > 0))(lambda: onward(k).start())

    @pl.when(me > 0)
    def _():
        to_below(0, ef).wait_send()
        to_below(1, ea).wait_send()
        to_above().wait_recv()

    @pl.when(me < n - 1)
    def _():
        to_above().wait_send()
        to_below(0, ef).wait_recv()
        to_below(1, ea).wait_recv()

    pl.when(first != me)(lambda: to_holder().wait_send())

    @pl.when((me >= 2) & (depth * (me - 2) < n))
    def _():
        @pl.loop(1, depth)
        def _(k):
            pl.when(depth * (me - 2) + k < n)(lambda: landed(k - 1).wait_recv())

    @pl.when((me >= 1) & (depth * (me - 1) < n))
    def _():
        @pl.loop(1, depth)
        def _(k):
            pl.when(depth * (me - 1) + k < n)(lambda: onward(k).wait_send())


def step_kernel(
    n,
    start_ref,
    amp_ref,
    source_ref,
    monitor_ref,
    ef_in,
    hf_in,
    pf_in,
    jf_in,
    ea_in,
    ha_in,
    pa_in,
    ja_in,
    below_in,
    above_in,
    slots_in,
    ef_out,
    hf_out,
    ea_out,
    ha_out,
    product_out,
    e,
    h,
    p,
    j,
    below,
    above,
    rho,
    drive,
    seen,
    product,
    en,
    hn,
    in_sem,
    out_sem,
    side_sem,
):
    me = lax.axis_index("gx")
    _, _, depth, nx, ny = e.shape
    start = start_ref[0]
    first_slot = 2 * depth - 1 - start
    sides = [
        pltpu.make_async_copy(below_in, below, side_sem.at[0]),
        pltpu.make_async_copy(slots_in.at[pl.ds(first_slot, depth)], rho, side_sem.at[1]),
        pltpu.make_async_copy(above_in, above, side_sem.at[2]),
    ]
    loads = {}
    pairs = ((e, ef_in, ea_in), (h, hf_in, ha_in), (j, jf_in, ja_in), (p, pf_in, pa_in))
    for l in range(depth):
        for k, (ref, *sources) in enumerate(pairs):
            for r, source in enumerate(sources):
                loads[k, l, r] = pltpu.make_async_copy(
                    source.at[:, l], ref.at[r, :, l], in_sem.at[k, l, r]
                )
    for r in range(2):
        loads[0, 0, r].start()
    for l in range(depth):
        for r in range(2):
            if l + 1 < depth:
                loads[0, l + 1, r].start()
            for k in (1, 2, 3):
                loads[k, l, r].start()
        if l == 0:
            sides[0].start()
            sides[1].start()
    sides[2].start()

    drive[...] = jnp.zeros_like(drive)
    seen[...] = jnp.zeros_like(seen)
    first_row = me * (depth * nx)
    lanes = lax.broadcasted_iota(jnp.int32, (1, ny), 1)

    @pl.loop(0, source_ref.shape[0])
    def _(s):
        cell = source_ref[s]
        row = cell // ny - first_row

        @pl.when((row >= 0) & (row < depth * nx))
        def _():
            hit = lanes == cell % ny
            for c in range(3):
                drive[c, pl.ds(row, 1), :] += jnp.where(hit, amp_ref[c, s], 0.0)

    @pl.loop(0, monitor_ref.shape[0])
    def _(s):
        cell = monitor_ref[s]
        row = cell // ny - first_row

        @pl.when((row >= 0) & (row < depth * nx))
        def _():
            seen[pl.ds(row, 1), :] += jnp.where(lanes == cell % ny, 1.0, 0.0)

    stores = []

    def store(source, dst, *index):
        copy = pltpu.make_async_copy(source, dst, out_sem.at[*index])
        copy.start()
        stores.append(copy)

    for r in range(2):
        loads[0, 0, r].wait()
    for l in range(depth):
        for r in range(2):
            if l + 1 < depth:
                loads[0, l + 1, r].wait()
            for k in (1, 2, 3):
                loads[k, l, r].wait()
        if l == 0:
            sides[0].wait()
            sides[1].wait()
        if l == depth - 1:
            sides[2].wait()
        owner = me * depth + l - start
        density = jnp.where((owner >= 0) & (owner < n), rho[l], 0.0)
        scale = DT / (1.0 + EPS_RANGE * density)
        strength = STRENGTH_BASE + STRENGTH_RANGE * density
        rows = pl.ds(l * nx, nx)
        old = new = None
        for r in range(2):
            ex, ey, ez = e[r, 0, l], e[r, 1, l], e[r, 2, l]
            if l + 1 < depth:
                ex_up, ey_up = e[r, 0, l + 1], e[r, 1, l + 1]
            else:
                ex_up = jnp.where(me < n - 1, above[r, 0], 0.0)
                ey_up = jnp.where(me < n - 1, above[r, 1], 0.0)
            hx = h[r, 0, l] - DT * ((ahead(ez, 1) - ez) - (ey_up - ey))
            hy = h[r, 1, l] - DT * ((ex_up - ex) - (ahead(ez, 0) - ez))
            hz = h[r, 2, l] - DT * ((ahead(ey, 0) - ey) - (ahead(ex, 1) - ex))
            hn[r, 0, l] = hx
            hn[r, 1, l] = hy
            hn[r, 2, l] = hz
            store(hn.at[r, :, l], (hf_out, ha_out)[r].at[:, l], 1, l, r)
            if l:
                hx_low, hy_low = hn[r, 0, l - 1], hn[r, 1, l - 1]
            else:
                hx_low = jnp.where(me > 0, below[r, 0] + DT * ey, 0.0)
                hy_low = jnp.where(me > 0, below[r, 1] - DT * ex, 0.0)
            curl = (
                (hz - behind(hz, 1)) - (hy - hy_low),
                (hx - hx_low) - (hz - behind(hz, 0)),
                (hy - behind(hy, 0)) - (hx - behind(hx, 1)),
            )
            fields = (ex, ey, ez)
            result = []
            for c in range(3):
                push = drive[c, rows, :] if r == 0 else seen[rows, :] * e[0, c, l]
                current = (
                    (1.0 - DAMPING * DT / 2.0) * j[r, c, l]
                    + DT * (strength * fields[c] - p[r, c, l])
                ) * (1.0 / (1.0 + DAMPING * DT / 2.0))
                result.append(fields[c] + scale * (curl[c] - current + push))
                en[r, c, l] = result[c]
            store(en.at[r, :, l], (ef_out, ea_out)[r].at[:, l], 0, l, r)
            if r == 0:
                old, new = fields, result
            else:
                product[l] = sum(
                    result[c] * ((new[c] - old[c]) + GAIN_FIELD * new[c]) for c in range(3)
                )
    last = pltpu.make_async_copy(
        product, product_out.at[pl.ds(first_slot, depth)], side_sem.at[3]
    )
    last.start()
    for copy in stores:
        copy.wait()
    last.wait()


def gradient_kernel(
    n,
    depth,
    radius_ref,
    start_ref,
    product_ref,
    grad_ref,
    arrived,
    own,
    relayed,
    load_sem,
    relay_send,
    relay_recv,
    send_sem,
    recv_sem,
    self_sem,
):
    me = lax.axis_index("gx")
    first = me // depth + 1
    base = depth * (me - 1)
    is_first = (me >= 1) & (base < n)
    is_second = (me >= 2) & (base - depth < n)
    load = pltpu.make_async_copy(product_ref.at[pl.ds(depth - 1, depth)], own, load_sem)
    pl.when(is_first)(lambda: load.start())

    barrier = pltpu.get_barrier_semaphore()

    def signal(device):
        pl.semaphore_signal(barrier, inc=1, device_id={"gx": device}, device_id_type=MESH)

    pl.when(first != me)(lambda: signal(first))
    pl.when(is_first)(lambda: signal(me + 1))
    owners = jnp.where(is_first, jnp.minimum(n - base, depth), 0)
    owners -= jnp.where(first == me, 1, 0)
    count = owners + jnp.where(is_second, 1, 0)
    pl.when(count > 0)(lambda: pl.semaphore_wait(barrier, count))

    def relay(k):
        return pltpu.make_async_remote_copy(
            src_ref=product_ref.at[k - 1],
            dst_ref=relayed.at[k],
            send_sem=relay_send.at[k],
            recv_sem=relay_recv.at[k],
            device_id={"gx": me - 1},
            device_id_type=MESH,
        )

    def back(k):
        return pltpu.make_async_remote_copy(
            src_ref=own.at[k],
            dst_ref=arrived,
            send_sem=send_sem.at[k],
            recv_sem=recv_sem,
            device_id={"gx": base + k},
            device_id_type=MESH,
        )

    def keep(k):
        return pltpu.make_async_copy(own.at[k], arrived, self_sem)

    @pl.when(is_second)
    def _():
        @pl.loop(1, depth)
        def _(k):
            pl.when(base - depth + k < n)(lambda: relay(k).start())

    @pl.when(is_first)
    def _():
        load.wait()
        for k in range(depth):

            @pl.when(base + k < n)
            def _():
                if k:
                    relay(k).wait_recv()
                    here = start_ref[0] + base + k < (me + 1) * depth
                    own[k] = jnp.where(here, own[k], relayed[k])
                pl.when(base + k != me)(lambda: back(k).start())
                pl.when(base + k == me)(lambda: keep(k).start())

    @pl.when(first != me)
    def _():
        back(0).wait_recv()

    @pl.when(first == me)
    def _():
        keep(0).wait()

    radius = radius_ref[0]
    plane = arrived[...]
    grad_ref[0] = band_product(plane * inverse_sums(plane.shape, radius), radius)

    @pl.when(is_second)
    def _():
        @pl.loop(1, depth)
        def _(k):
            pl.when(base - depth + k < n)(lambda: relay(k).wait_send())

    @pl.when(is_first)
    def _():
        @pl.loop(0, depth)
        def _(k):
            pl.when((base + k < n) & (base + k != me))(lambda: back(k).wait_send())


def body(
    n,
    e_forward,
    h_forward,
    p_forward,
    j_forward,
    e_adjoint,
    h_adjoint,
    p_adjoint,
    j_adjoint,
    design,
    source_amp,
    source_cell,
    monitor_cell,
    slab_start,
    radius,
):
    _, depth, nx, ny = e_forward.shape
    slots = 2 * depth - 1
    dma = pltpu.SemaphoreType.DMA
    below, above, densities = pl.pallas_call(
        functools.partial(exchange_kernel, n),
        out_shape=(
            jax.ShapeDtypeStruct((2, 2, nx, ny), F32),
            jax.ShapeDtypeStruct((2, 2, nx, ny), F32),
            jax.ShapeDtypeStruct((slots, nx, ny), F32),
        ),
        in_specs=[SMEM, VMEM, HBM, HBM, HBM, HBM],
        out_specs=(HBM, HBM, HBM),
        scratch_shapes=[
            pltpu.VMEM((2, 3, nx, ny), F32),
            pltpu.VMEM((2, 2, nx, ny), F32),
            pltpu.VMEM((2, 2, nx, ny), F32),
            pltpu.VMEM((nx, ny), F32),
            dma((2, 2)),
            dma(()),
            dma((depth,)),
            dma(()),
            dma(()),
            dma((2,)),
            dma((2,)),
            dma((slots,)),
            dma(()),
        ],
        compiler_params=pltpu.CompilerParams(
            collective_id=0, has_side_effects=True, vmem_limit_bytes=BIG
        ),
        name="exchange",
    )(radius, design, e_forward, e_adjoint, h_forward, h_adjoint)
    field = jax.ShapeDtypeStruct(e_forward.shape, F32)
    both = pltpu.VMEM((2,) + e_forward.shape, F32)
    ef, hf, ea, ha, product = pl.pallas_call(
        functools.partial(step_kernel, n),
        out_shape=(field, field, field, field, jax.ShapeDtypeStruct((slots, nx, ny), F32)),
        in_specs=[SMEM] * 4 + [HBM] * 11,
        out_specs=(HBM,) * 5,
        scratch_shapes=[
            both,
            both,
            both,
            both,
            pltpu.VMEM((2, 2, nx, ny), F32),
            pltpu.VMEM((2, 2, nx, ny), F32),
            pltpu.VMEM((depth, nx, ny), F32),
            pltpu.VMEM((3, depth * nx, ny), F32),
            pltpu.VMEM((depth * nx, ny), F32),
            pltpu.VMEM((depth, nx, ny), F32),
            both,
            both,
            dma((4, depth, 2)),
            dma((2, depth, 2)),
            dma((4,)),
        ],
        compiler_params=pltpu.CompilerParams(vmem_limit_bytes=BIG),
        name="step",
    )(
        slab_start,
        source_amp.T,
        source_cell,
        monitor_cell,
        e_forward,
        h_forward,
        p_forward,
        j_forward,
        e_adjoint,
        h_adjoint,
        p_adjoint,
        j_adjoint,
        below,
        above,
        densities,
    )
    grad = pl.pallas_call(
        functools.partial(gradient_kernel, n, depth),
        out_shape=jax.ShapeDtypeStruct(design.shape, F32),
        in_specs=[SMEM, SMEM, HBM],
        out_specs=VMEM,
        scratch_shapes=[
            pltpu.VMEM((nx, ny), F32),
            pltpu.VMEM((depth, nx, ny), F32),
            pltpu.VMEM((depth, nx, ny), F32),
            dma(()),
            dma((depth,)),
            dma((depth,)),
            dma((depth,)),
            dma(()),
            dma(()),
        ],
        compiler_params=pltpu.CompilerParams(
            collective_id=1, has_side_effects=True, vmem_limit_bytes=BIG
        ),
        name="gradient",
    )(radius, slab_start, product)
    return ef, hf, ea, ha, grad


def solution(mesh):
    field = P(None, ("grp", "gx"), None, None)
    plane = P(("grp", "gx"), None, None)
    return jax.shard_map(
        functools.partial(body, mesh.shape["gx"]),
        mesh=mesh,
        in_specs=(field,) * 8 + (plane, P("grp", None)) + (P("grp"),) * 4,
        out_specs=(field,) * 4 + (plane,),
        check_vma=False,
    )
```

```python
import functools

import jax
import jax.numpy as jnp
from jax import lax
from jax.experimental import pallas as pl
from jax.experimental.pallas import tpu as pltpu
from jax.sharding import PartitionSpec as P

DT = 0.5
EPS_RANGE = 10.0
STRENGTH_BASE = 0.5
STRENGTH_RANGE = 3.0
DAMPING = 0.2
GAIN_FIELD = 0.25
BIG = 60 * 1024 * 1024
SMALL = 6 * 1024 * 1024
CHUNK = 2
MESH = pl.DeviceIdType.MESH
F32 = jnp.float32
BF16 = jnp.bfloat16
HBM = pl.BlockSpec(memory_space=pltpu.HBM)
SMEM = pl.BlockSpec(memory_space=pltpu.SMEM)
VMEM = pl.BlockSpec(memory_space=pltpu.VMEM)


def slot_range(me, n, depth):
    base = depth * (me - 1) - (depth - 1)
    return base, jnp.maximum(base, 0), jnp.minimum(base + 2 * depth - 1, n)


def holders(me, depth):
    first = me // depth + 1
    return first, first + 1, me % depth


def ahead(v, axis):
    size = v.shape[axis]
    pos = lax.broadcasted_iota(jnp.int32, v.shape, axis)
    return jnp.where(pos == size - 1, 0.0, pltpu.roll(v, size - 1, axis))


def behind(v, axis):
    pos = lax.broadcasted_iota(jnp.int32, v.shape, axis)
    return jnp.where(pos == 0, 0.0, pltpu.roll(v, 1, axis))


def triangle(size, radius):
    a = lax.broadcasted_iota(jnp.int32, (size, size), 0)
    b = lax.broadcasted_iota(jnp.int32, (size, size), 1)
    return jnp.maximum(radius + 1 - jnp.abs(a - b), 0).astype(F32).astype(BF16)


def row_sums(shape, axis, radius):
    pos = lax.broadcasted_iota(jnp.int32, shape, axis)
    low = jnp.maximum(radius - pos, 0)
    high = jnp.maximum(radius - (shape[axis] - 1 - pos), 0)
    whole = (radius + 1) * (radius + 1)
    low, high = low.astype(F32), high.astype(F32)
    return whole.astype(F32) - 0.5 * (low * (low + 1.0) + high * (high + 1.0))


def halves(v):
    big = v.astype(BF16)
    return big, (v - big.astype(F32)).astype(BF16)


def band_product(plane, radius):
    nx, ny = plane.shape
    tx, ty = triangle(nx, radius), triangle(ny, radius)
    big, small = halves(plane)
    both = jnp.dot(jnp.concatenate([big, small], 0), ty, preferred_element_type=F32)
    big, small = halves(both[:nx] + both[nx:])
    return jnp.dot(tx, big, preferred_element_type=F32) + jnp.dot(
        tx, small, preferred_element_type=F32
    )


def inverse_sums(shape, radius):
    return 1.0 / (row_sums(shape, 0, radius) * row_sums(shape, 1, radius))


def exchange_kernel(
    n,
    radius_ref,
    design_ref,
    ef,
    ea,
    hf,
    ha,
    below_ref,
    above_ref,
    slots_ref,
    eb,
    hb,
    part,
    rho,
    load_sem,
    send_sem,
    up_send,
    up_recv,
    down_send,
    down_recv,
    slot_recv,
    self_sem,
):
    me = lax.axis_index("gx")
    depth = ef.shape[1]
    loads = []
    for r, (e, h) in enumerate(((ef, hf), (ea, ha))):
        loads.append(pltpu.make_async_copy(e.at[:, depth - 1], eb.at[r], load_sem.at[r, 0]))
        loads.append(pltpu.make_async_copy(h.at[0:2, depth - 1], hb.at[r], load_sem.at[r, 1]))
    for load in loads:
        load.start()

    barrier = pltpu.get_barrier_semaphore()

    @pl.loop(1, n)
    def _(k):
        pl.semaphore_signal(
            barrier, inc=1, device_id={"gx": lax.rem(me + k, n)}, device_id_type=MESH
        )

    radius = radius_ref[0]
    plane = design_ref[0]
    rho[...] = band_product(plane, radius) * inverse_sums(plane.shape, radius)
    pl.semaphore_wait(barrier, n - 1)

    first, second, shift = holders(me, depth)

    def to_holder(which, holder):
        slot = me - (depth * (holder - 1) - (depth - 1))
        return pltpu.make_async_remote_copy(
            src_ref=rho,
            dst_ref=slots_ref.at[slot],
            send_sem=send_sem.at[which],
            recv_sem=slot_recv.at[slot],
            device_id={"gx": holder},
            device_id_type=MESH,
        )

    def to_self(holder):
        slot = me - (depth * (holder - 1) - (depth - 1))
        return pltpu.make_async_copy(rho, slots_ref.at[slot], self_sem)

    def each_holder(remote, local):
        for which, holder, used in ((0, first, shift >= 0), (1, second, shift != 0)):
            pl.when(used & (holder != me))(functools.partial(remote, which, holder))
            pl.when(used & (holder == me))(functools.partial(local, holder))

    def to_below(r, e):
        return pltpu.make_async_remote_copy(
            src_ref=e.at[0:2, 0],
            dst_ref=above_ref.at[r],
            send_sem=down_send.at[r],
            recv_sem=down_recv.at[r],
            device_id={"gx": me - 1},
            device_id_type=MESH,
        )

    def to_above():
        return pltpu.make_async_remote_copy(
            src_ref=part,
            dst_ref=below_ref,
            send_sem=up_send,
            recv_sem=up_recv,
            device_id={"gx": me + 1},
            device_id_type=MESH,
        )

    each_holder(
        lambda which, holder: to_holder(which, holder).start(),
        lambda holder: to_self(holder).start(),
    )

    @pl.when(me > 0)
    def _():
        to_below(0, ef).start()
        to_below(1, ea).start()

    for load in loads:
        load.wait()
    for r in range(2):
        ex, ey, ez = eb[r, 0], eb[r, 1], eb[r, 2]
        part[r, 0] = hb[r, 0] - DT * (ahead(ez, 1) - ez + ey)
        part[r, 1] = hb[r, 1] + DT * (ex + (ahead(ez, 0) - ez))

    @pl.when(me < n - 1)
    def _():
        to_above().start()

    each_holder(
        lambda which, holder: to_holder(which, holder).wait_send(),
        lambda holder: to_self(holder).wait(),
    )

    @pl.when(me > 0)
    def _():
        to_below(0, ef).wait_send()
        to_below(1, ea).wait_send()
        to_above().wait_recv()

    @pl.when(me < n - 1)
    def _():
        to_above().wait_send()
        to_below(0, ef).wait_recv()
        to_below(1, ea).wait_recv()

    base, low, high = slot_range(me, n, depth)

    @pl.loop(low, high)
    def _(owner):
        @pl.when(owner != me)
        def _():
            pltpu.make_async_remote_copy(
                src_ref=rho,
                dst_ref=slots_ref.at[owner - base],
                send_sem=send_sem.at[0],
                recv_sem=slot_recv.at[owner - base],
                device_id={"gx": owner},
                device_id_type=MESH,
            ).wait_recv()


def step_kernel(
    n,
    start_ref,
    amp_ref,
    source_ref,
    monitor_ref,
    ef_in,
    hf_in,
    pf_in,
    jf_in,
    ea_in,
    ha_in,
    pa_in,
    ja_in,
    below_in,
    above_in,
    slots_in,
    ef_out,
    hf_out,
    ea_out,
    ha_out,
    product_out,
    e,
    h,
    p,
    j,
    below,
    above,
    rho,
    drive,
    seen,
    product,
    en,
    hn,
    in_sem,
    out_sem,
    side_sem,
):
    me = lax.axis_index("gx")
    _, _, depth, nx, ny = e.shape
    start = start_ref[0]
    first_slot = 2 * depth - 1 - start
    sides = [
        pltpu.make_async_copy(below_in, below, side_sem.at[0]),
        pltpu.make_async_copy(slots_in.at[pl.ds(first_slot, depth)], rho, side_sem.at[1]),
        pltpu.make_async_copy(above_in, above, side_sem.at[2]),
    ]
    loads = {}
    pairs = ((e, ef_in, ea_in), (h, hf_in, ha_in), (j, jf_in, ja_in), (p, pf_in, pa_in))
    for l in range(0, depth, CHUNK):
        part = pl.ds(l, CHUNK)
        for k, (ref, *sources) in enumerate(pairs):
            for r, source in enumerate(sources):
                loads[k, l, r] = pltpu.make_async_copy(
                    source.at[:, part], ref.at[r, :, part], in_sem.at[k, l, r]
                )
    for r in range(2):
        loads[0, 0, r].start()
    for l in range(0, depth, CHUNK):
        for r in range(2):
            if l + CHUNK < depth:
                loads[0, l + CHUNK, r].start()
            for k in (1, 2, 3):
                loads[k, l, r].start()
        if l == 0:
            sides[0].start()
            sides[1].start()
    sides[2].start()

    drive[...] = jnp.zeros_like(drive)
    seen[...] = jnp.zeros_like(seen)
    first_row = me * (depth * nx)
    lanes = lax.broadcasted_iota(jnp.int32, (1, ny), 1)

    @pl.loop(0, source_ref.shape[0])
    def _(s):
        cell = source_ref[s]
        row = cell // ny - first_row

        @pl.when((row >= 0) & (row < depth * nx))
        def _():
            hit = lanes == cell % ny
            for c in range(3):
                drive[c, pl.ds(row, 1), :] += jnp.where(hit, amp_ref[c, s], 0.0)

    @pl.loop(0, monitor_ref.shape[0])
    def _(s):
        cell = monitor_ref[s]
        row = cell // ny - first_row

        @pl.when((row >= 0) & (row < depth * nx))
        def _():
            seen[pl.ds(row, 1), :] += jnp.where(lanes == cell % ny, 1.0, 0.0)

    stores = []

    def store(source, dst, *index):
        copy = pltpu.make_async_copy(source, dst, out_sem.at[*index])
        copy.start()
        stores.append(copy)

    for r in range(2):
        loads[0, 0, r].wait()
    for l in range(depth):
        for r in range(2):
            if (0, l + 1, r) in loads:
                loads[0, l + 1, r].wait()
            for k in (1, 2, 3):
                if (k, l, r) in loads:
                    loads[k, l, r].wait()
        if l == 0:
            sides[0].wait()
            sides[1].wait()
        if l == depth - 1:
            sides[2].wait()
        owner = me * depth + l - start
        density = jnp.where((owner >= 0) & (owner < n), rho[l], 0.0)
        scale = DT / (1.0 + EPS_RANGE * density)
        strength = STRENGTH_BASE + STRENGTH_RANGE * density
        rows = pl.ds(l * nx, nx)
        old = new = None
        for r in range(2):
            ex, ey, ez = e[r, 0, l], e[r, 1, l], e[r, 2, l]
            if l + 1 < depth:
                ex_up, ey_up = e[r, 0, l + 1], e[r, 1, l + 1]
            else:
                ex_up = jnp.where(me < n - 1, above[r, 0], 0.0)
                ey_up = jnp.where(me < n - 1, above[r, 1], 0.0)
            hx = h[r, 0, l] - DT * ((ahead(ez, 1) - ez) - (ey_up - ey))
            hy = h[r, 1, l] - DT * ((ex_up - ex) - (ahead(ez, 0) - ez))
            hz = h[r, 2, l] - DT * ((ahead(ey, 0) - ey) - (ahead(ex, 1) - ex))
            hn[r, 0, l] = hx
            hn[r, 1, l] = hy
            hn[r, 2, l] = hz
            done = pl.ds(l - CHUNK + 1, CHUNK)
            if (l + 1) % CHUNK == 0:
                store(hn.at[r, :, done], (hf_out, ha_out)[r].at[:, done], 1, l, r)
            if l:
                hx_low, hy_low = hn[r, 0, l - 1], hn[r, 1, l - 1]
            else:
                hx_low = jnp.where(me > 0, below[r, 0] + DT * ey, 0.0)
                hy_low = jnp.where(me > 0, below[r, 1] - DT * ex, 0.0)
            curl = (
                (hz - behind(hz, 1)) - (hy - hy_low),
                (hx - hx_low) - (hz - behind(hz, 0)),
                (hy - behind(hy, 0)) - (hx - behind(hx, 1)),
            )
            fields = (ex, ey, ez)
            result = []
            for c in range(3):
                push = drive[c, rows, :] if r == 0 else seen[rows, :] * e[0, c, l]
                current = (
                    (1.0 - DAMPING * DT / 2.0) * j[r, c, l]
                    + DT * (strength * fields[c] - p[r, c, l])
                ) * (1.0 / (1.0 + DAMPING * DT / 2.0))
                result.append(fields[c] + scale * (curl[c] - current + push))
                en[r, c, l] = result[c]
            if (l + 1) % CHUNK == 0:
                store(en.at[r, :, done], (ef_out, ea_out)[r].at[:, done], 0, l, r)
            if r == 0:
                old, new = fields, result
            else:
                product[l] = sum(
                    result[c] * ((new[c] - old[c]) + GAIN_FIELD * new[c]) for c in range(3)
                )
    last = pltpu.make_async_copy(
        product, product_out.at[pl.ds(first_slot, depth)], side_sem.at[3]
    )
    last.start()
    for copy in stores:
        copy.wait()
    last.wait()


def gradient_kernel(
    n,
    depth,
    radius_ref,
    start_ref,
    product_ref,
    grad_ref,
    arrived,
    send_sem,
    recv_sem,
    self_sem,
):
    me = lax.axis_index("gx")
    first, second, shift = holders(me, depth)
    base, low, high = slot_range(me, n, depth)
    barrier = pltpu.get_barrier_semaphore()
    for holder, used in ((first, shift >= 0), (second, shift != 0)):

        @pl.when(used & (holder != me))
        def _():
            pl.semaphore_signal(barrier, inc=1, device_id={"gx": holder}, device_id_type=MESH)

    inside = jnp.where((me >= low) & (me < high), 1, 0)
    count = jnp.maximum(high - low, 0) - inside

    @pl.when(count > 0)
    def _():
        pl.semaphore_wait(barrier, count)

    def back(owner):
        slot = owner - base
        which = jnp.where(slot >= depth - 1, 0, 1)
        return pltpu.make_async_remote_copy(
            src_ref=product_ref.at[slot],
            dst_ref=arrived.at[which],
            send_sem=send_sem.at[slot],
            recv_sem=recv_sem.at[which],
            device_id={"gx": owner},
            device_id_type=MESH,
        )

    def keep():
        slot = me - base
        which = jnp.where(slot >= depth - 1, 0, 1)
        return pltpu.make_async_copy(product_ref.at[slot], arrived.at[which], self_sem)

    @pl.loop(low, high)
    def _(owner):
        pl.when(owner != me)(lambda: back(owner).start())
        pl.when(owner == me)(lambda: keep().start())

    for which, holder, used in ((0, first, shift >= 0), (1, second, shift != 0)):

        @pl.when(used & (holder != me))
        def _():
            pltpu.make_async_remote_copy(
                src_ref=product_ref.at[0],
                dst_ref=arrived.at[which],
                send_sem=send_sem.at[0],
                recv_sem=recv_sem.at[which],
                device_id={"gx": holder},
                device_id_type=MESH,
            ).wait_recv()

        pl.when(used & (holder == me))(lambda: keep().wait())

    radius = radius_ref[0]
    in_first = start_ref[0] + me < (first + 1) * depth
    plane = jnp.where(in_first, arrived[0], arrived[1])
    grad_ref[0] = band_product(plane * inverse_sums(plane.shape, radius), radius)

    @pl.loop(low, high)
    def _(owner):
        pl.when(owner != me)(lambda: back(owner).wait_send())


def body(
    n,
    e_forward,
    h_forward,
    p_forward,
    j_forward,
    e_adjoint,
    h_adjoint,
    p_adjoint,
    j_adjoint,
    design,
    source_amp,
    source_cell,
    monitor_cell,
    slab_start,
    radius,
):
    _, depth, nx, ny = e_forward.shape
    slots = 2 * depth - 1
    dma = pltpu.SemaphoreType.DMA
    below, above, densities = pl.pallas_call(
        functools.partial(exchange_kernel, n),
        out_shape=(
            jax.ShapeDtypeStruct((2, 2, nx, ny), F32),
            jax.ShapeDtypeStruct((2, 2, nx, ny), F32),
            jax.ShapeDtypeStruct((slots, nx, ny), F32),
        ),
        in_specs=[SMEM, VMEM, HBM, HBM, HBM, HBM],
        out_specs=(HBM, HBM, HBM),
        scratch_shapes=[
            pltpu.VMEM((2, 3, nx, ny), F32),
            pltpu.VMEM((2, 2, nx, ny), F32),
            pltpu.VMEM((2, 2, nx, ny), F32),
            pltpu.VMEM((nx, ny), F32),
            dma((2, 2)),
            dma((2,)),
            dma(()),
            dma(()),
            dma((2,)),
            dma((2,)),
            dma((slots,)),
            dma(()),
        ],
        compiler_params=pltpu.CompilerParams(
            collective_id=0, has_side_effects=True, vmem_limit_bytes=BIG
        ),
        name="exchange",
    )(radius, design, e_forward, e_adjoint, h_forward, h_adjoint)
    field = jax.ShapeDtypeStruct(e_forward.shape, F32)
    both = pltpu.VMEM((2,) + e_forward.shape, F32)
    ef, hf, ea, ha, product = pl.pallas_call(
        functools.partial(step_kernel, n),
        out_shape=(field, field, field, field, jax.ShapeDtypeStruct((slots, nx, ny), F32)),
        in_specs=[SMEM] * 4 + [HBM] * 11,
        out_specs=(HBM,) * 5,
        scratch_shapes=[
            both,
            both,
            both,
            both,
            pltpu.VMEM((2, 2, nx, ny), F32),
            pltpu.VMEM((2, 2, nx, ny), F32),
            pltpu.VMEM((depth, nx, ny), F32),
            pltpu.VMEM((3, depth * nx, ny), F32),
            pltpu.VMEM((depth * nx, ny), F32),
            pltpu.VMEM((depth, nx, ny), F32),
            both,
            both,
            dma((4, depth, 2)),
            dma((2, depth, 2)),
            dma((4,)),
        ],
        compiler_params=pltpu.CompilerParams(vmem_limit_bytes=BIG),
        name="step",
    )(
        slab_start,
        source_amp.T,
        source_cell,
        monitor_cell,
        e_forward,
        h_forward,
        p_forward,
        j_forward,
        e_adjoint,
        h_adjoint,
        p_adjoint,
        j_adjoint,
        below,
        above,
        densities,
    )
    grad = pl.pallas_call(
        functools.partial(gradient_kernel, n, depth),
        out_shape=jax.ShapeDtypeStruct(design.shape, F32),
        in_specs=[SMEM, SMEM, HBM],
        out_specs=VMEM,
        scratch_shapes=[
            pltpu.VMEM((2, nx, ny), F32),
            dma((slots,)),
            dma((2,)),
            dma(()),
        ],
        compiler_params=pltpu.CompilerParams(
            collective_id=1, has_side_effects=True, vmem_limit_bytes=SMALL
        ),
        name="gradient",
    )(radius, slab_start, product)
    return ef, hf, ea, ha, grad


def solution(mesh):
    field = P(None, ("grp", "gx"), None, None)
    plane = P(("grp", "gx"), None, None)
    return jax.shard_map(
        functools.partial(body, mesh.shape["gx"]),
        mesh=mesh,
        in_specs=(field,) * 8 + (plane, P("grp", None)) + (P("grp"),) * 4,
        out_specs=(field,) * 4 + (plane,),
        check_vma=False,
    )
```
